256 devices in a mesh: section: 8 (over y, x_lo), fsdp: 32 (over x_hi, z, core).
Axes of the slice: x: 4 (x_hi: 2, x_lo: 2; x = x_hi * 2 + x_lo), y: 4, z: 8, core: 2. Of those that a mesh axis runs over, the one named last changes fastest.
Arguments:
- hidden: bfloat16 [2, 32, 192, 2048], P(None, 'fsdp'), may hold values from -20 to 20
- pool_states: bfloat16 [256, 128, 512], P('fsdp', 'section'), may hold values from -6 to 6
- neighbour_ids: int32 [2, 32, 3, 2], P(None, 'fsdp'), may hold values from 0 to 255
- batch_order: int32 [2], replicated, may hold values from 0 to 1, each once
- key_weight: bfloat16 [8, 512, 2048], P('section', 'fsdp'), may hold values from -0.25 to 0.25
- value_weight: bfloat16 [8, 512, 2048], P('section', 'fsdp'), may hold values from -0.25 to 0.25
- query_gain: float32 [8, 2048], P('section'), may hold values from 0.5 to 2
Outputs:
- output: bfloat16 [2, 32, 192, 2048], P(None, 'fsdp', None, 'section')
The draws below stay inside these ranges and needn't reach their ends.
Inputs may be any that keep to these rules, and one draw needn't show every extreme that they name: `batch_order`: each of the 2 micro-batches once.
All inputs are finite; a program needn't handle non-finite values.
Results may differ from the reference program's by a relative error of at most 0.0078.
Values may be sent and summed in bfloat16 or wider, within the bound.
No kernel may reach another device: no remote copies, remote signals or barrier semaphores. Data moves between devices by JAX's collectives and lax.ppermute only.
A program may use at most 192 MiB of HBM per device.

```python
import math
import jax
import jax.numpy as jnp
from jax import lax

HEAD_COUNT = 16
HEAD_DIM = 128
ENC_WIDTH = 512
SPAN_LEN = 64
NEIGHBOURS = 2
NEIGH_LEN = 128
SPAN_COUNT = 3
MICRO_BATCHES = 2
FEATURES = 2048
SEQ_LEN = 192
SEQUENCES = 32
POOL_SIZE = 256
LAYERS = 8


def draw_hidden(key, part):
    key = jax.random.fold_in(key, 11)
    entry_key, row_key, column_key = jax.random.split(key, 3)
    full_shape = (MICRO_BATCHES, SEQUENCES, SEQ_LEN, FEATURES)
    row_shape = (MICRO_BATCHES, SEQUENCES, SEQ_LEN, 1)
    entries = jax.random.truncated_normal(entry_key, -4.0, 4.0, full_shape, jnp.float32)
    row_scale = jnp.exp(jax.random.uniform(row_key, row_shape, jnp.float32, math.log(0.4), math.log(2.5)))
    column_scale = jnp.exp(jax.random.uniform(column_key, (FEATURES,), jnp.float32, math.log(0.5), math.log(2.0)))
    return (entries * row_scale * column_scale).astype(jnp.bfloat16)


def place_ends(values, rng, least, high):
    dims = values.shape
    spot = [jax.random.randint(jax.random.fold_in(rng, axis), (), 0, dims[axis]) for axis in range(len(dims))]
    values = values.at[tuple(spot)].set(least)
    longest = dims.index(max(dims))
    spot[longest] = (spot[longest] + 1) % dims[longest]
    return values.at[tuple(spot)].set(high)


def block_levels(stream_key, shape, cuts, least, high):
    factor_of, own = 1.0, jax.random.fold_in(stream_key, 6)
    for axis_at, shards_of in cuts:
        draws = jnp.exp(jax.random.uniform(jax.random.fold_in(own, axis_at), (shards_of,), jnp.float32, least / len(cuts), high / len(cuts)))
        factor_of = factor_of * jnp.repeat(draws, shape[axis_at] // shards_of).reshape([-1 if axis == axis_at else 1 for axis in range(len(shape))])
    return factor_of


def gaussian(stream_key, extent, deviation, reach, shards=(), held_as=jnp.bfloat16):
    level = block_levels(stream_key, extent, shards, -0.22, 0.18) if shards else 1.0
    values = jax.random.normal(stream_key, extent, jnp.float32) * deviation * level
    return jnp.minimum(jnp.maximum(values, -reach), reach).astype(held_as)


def setup_inputs(seed: int = 0) -> dict:
    keys = jax.random.split(jax.random.key(seed), 8)
    return {
        "hidden": draw_hidden(jax.random.fold_in(keys[7], 71), 0),
        "pool_states": gaussian(keys[1], (POOL_SIZE, NEIGH_LEN, ENC_WIDTH), 1.0, 6.0, ((0, 32), (1, 8))),
        "neighbour_ids": place_ends(jax.random.randint(keys[2], (MICRO_BATCHES, SEQUENCES, SPAN_COUNT, NEIGHBOURS), 0, POOL_SIZE), jax.random.fold_in(keys[2], 1), 0, POOL_SIZE - 1).astype(jnp.int32),
        "batch_order": jax.random.permutation(keys[3], MICRO_BATCHES).astype(jnp.int32),
        "key_weight": gaussian(keys[4], (LAYERS, ENC_WIDTH, FEATURES), ENC_WIDTH ** -0.5, 0.25, ((0, 8), (1, 32))),
        "value_weight": gaussian(keys[5], (LAYERS, ENC_WIDTH, FEATURES), ENC_WIDTH ** -0.5, 0.25, ((0, 8), (1, 32))),
        "query_gain": jnp.clip(jnp.exp(math.log(2.0) - 1.3862944 * jax.random.uniform(keys[6], (LAYERS, FEATURES), jnp.float32) ** block_levels(keys[6], (LAYERS, FEATURES), ((0, 8),), -0.2, 0.2)), 0.5, 2.0),
    }


EPSILON = 1e-06

def rms_scale(values):
    return values * lax.rsqrt(lax.optimization_barrier(jnp.mean(values * values, axis=-1, keepdims=True)) + EPSILON)

def cross_attend(current, key_block, value_block, gain_row):
    offset = SPAN_LEN - 1
    feature_count = current.shape[-1]
    widened = current.astype(jnp.float32)
    queries = (rms_scale(widened) * gain_row).astype(jnp.bfloat16)
    shifted = jnp.concatenate([queries[offset:], jnp.zeros((offset, feature_count), jnp.bfloat16)], axis=0)
    grouped = shifted.reshape(SPAN_COUNT, SPAN_LEN, HEAD_COUNT, HEAD_DIM).astype(jnp.float32)
    key_heads = key_block.reshape(SPAN_COUNT, NEIGHBOURS * NEIGH_LEN, HEAD_COUNT, HEAD_DIM).astype(jnp.float32)
    value_heads = value_block.reshape(SPAN_COUNT, NEIGHBOURS * NEIGH_LEN, HEAD_COUNT, HEAD_DIM).astype(jnp.float32)
    scores = jnp.einsum('cqhd,ckhd->chqk', grouped, key_heads) * HEAD_DIM ** (-0.5)
    expanded = jnp.exp(scores)
    attention = (expanded / lax.optimization_barrier(jnp.sum(expanded, axis=-1, keepdims=True))).astype(jnp.bfloat16)
    mixture = jnp.einsum('chqk,ckhd->cqhd', attention.astype(jnp.float32), value_heads)
    mixture = mixture.reshape(SPAN_COUNT * SPAN_LEN, feature_count)
    update = jnp.concatenate([jnp.zeros((offset, feature_count), jnp.float32), mixture[:SPAN_COUNT * SPAN_LEN - offset]], axis=0)
    return (widened + update).astype(jnp.bfloat16)

def reference(hidden, pool_states, neighbour_ids, batch_order, key_weight, value_weight, query_gain):
    joined = jnp.concatenate([key_weight, value_weight], axis=2).astype(jnp.float32)

    def one_sequence(inputs):
        current, chosen = inputs
        gathered = jnp.take(pool_states, chosen, axis=0).astype(jnp.float32)
        rounded = rms_scale(gathered).astype(jnp.bfloat16)
        rounded = lax.optimization_barrier(rounded)
        encoded = rounded.astype(jnp.float32).reshape(SPAN_COUNT, NEIGHBOURS * NEIGH_LEN, ENC_WIDTH)
        for layer_index in range(LAYERS):
            projected = jnp.einsum('cne,ef->cnf', encoded, joined[layer_index]).astype(jnp.bfloat16)
            key_block = projected[:, :, :FEATURES]
            value_block = projected[:, :, FEATURES:]
            current = cross_attend(current, key_block, value_block, query_gain[layer_index])
        return current
    ordered = jnp.take(hidden, batch_order, axis=0).reshape(MICRO_BATCHES * SEQUENCES, SEQ_LEN, FEATURES)
    chosen_all = jnp.take(neighbour_ids, batch_order, axis=0).reshape(MICRO_BATCHES * SEQUENCES, SPAN_COUNT * NEIGHBOURS)
    finished = lax.map(one_sequence, (ordered, chosen_all))
    return finished.reshape(MICRO_BATCHES, SEQUENCES, SEQ_LEN, FEATURES)
```

```python
import functools

import jax
import jax.numpy as jnp
from jax import lax
from jax.experimental import pallas as pl
from jax.experimental.pallas import tpu as pltpu
from jax.sharding import Mesh
from jax.sharding import PartitionSpec as P

HEAD_DIM = 128
SPAN_LEN = 64
LAYERS = 8
FEATURES = 2048
SLICE = 256
ACTIVE = 128
EPSILON = 1e-06
FIRST = SPAN_LEN - 1
EARLY = 4

AXES = ("yh", "yl", "xl", "xh", "z", "c")
SIZES = (2, 2, 2, 2, 8, 2)
SECTION = ("yh", "yl", "xl")
FSDP = ("xh", "z", "c")
SWAP = [(0, 1), (1, 0)]


def swapped(block, axis):
    return lax.ppermute(block, axis, SWAP)


def shifted(block, axis, size, distance):
    return lax.ppermute(block, axis, [(i, (i + distance) % size) for i in range(size)])


def quad(block):
    axis = ("yl", "xl")
    return [lax.ppermute(block, axis, [(i, i ^ d) for i in range(4)]) for d in (1, 2, 3)]


def ring_gather(block, z):
    held = jnp.zeros((8,) + block.shape, block.dtype)
    held = lax.dynamic_update_index_in_dim(held, block, z, 0)
    for d in (4, 3, -3, 2, -2, 1, -1):
        held = lax.dynamic_update_index_in_dim(held, shifted(block, "z", 8, d), (z - d) % 8, 0)
    return held


def kv_kernel(core_ref, enc_ref, mine_ref, other_ref, key_ref, value_ref, held, sems, *, layer):
    core = core_ref[0]
    copies = []
    for which, source in enumerate((mine_ref, other_ref)):
        slot = core if which == 0 else 1 - core
        for kv in range(2):
            for xh in range(2):
                copies.append(
                    pltpu.make_async_copy(
                        source.at[:, layer, kv, xh], held.at[kv, xh, :, slot], sems.at[which, kv, xh]
                    )
                )
    for copy in copies:
        copy.start()
    for copy in copies:
        copy.wait()
    keys = held[0].reshape(512, 512)
    values = held[1].reshape(512, 512)
    for g in range(3):
        tokens = enc_ref[:, :, 2 * g : 2 * g + 2].reshape(256, 512)
        key_ref[g] = jnp.dot(tokens, keys, preferred_element_type=jnp.float32).astype(jnp.bfloat16)
        made = jnp.dot(tokens, values, preferred_element_type=jnp.float32)
        value_ref[g] = made.T.astype(jnp.bfloat16)


def make_kv(core, encoded, mine, other, layer):
    vmem = pl.BlockSpec(memory_space=pltpu.VMEM)
    return pl.pallas_call(
        functools.partial(kv_kernel, layer=layer),
        out_shape=(
            jax.ShapeDtypeStruct((3, 256, 512), jnp.bfloat16),
            jax.ShapeDtypeStruct((3, 512, 256), jnp.bfloat16),
        ),
        in_specs=[
            pl.BlockSpec(memory_space=pltpu.SMEM),
            vmem,
            pl.BlockSpec(memory_space=pl.ANY),
            pl.BlockSpec(memory_space=pl.ANY),
        ],
        out_specs=(vmem, vmem),
        scratch_shapes=[
            pltpu.VMEM((2, 2, 8, 2, 16, 512), jnp.bfloat16),
            pltpu.SemaphoreType.DMA((2, 2, 2)),
        ],
        compiler_params=pltpu.CompilerParams(vmem_limit_bytes=24 << 20),
        cost_estimate=pl.CostEstimate(
            flops=2 * 768 * 512 * 1024, bytes_accessed=4 << 20, transcendentals=0
        ),
        name="kv",
    )(core, encoded, mine, other)


def layer_kernel(cur_ref, one_ref, s0_ref, s1_ref, s2_ref, s3_ref, key_ref, value_ref, *outs, last):
    total = s0_ref[...] + s1_ref[...] + s2_ref[...] + s3_ref[...]
    scale = lax.rsqrt(total * (1.0 / FEATURES) + EPSILON) * HEAD_DIM ** (-0.5)
    left = lax.broadcasted_iota(jnp.int32, (1, ACTIVE), 1) < SPAN_LEN
    squares = jnp.zeros((1, ACTIVE), jnp.float32)
    for h in range(4):
        rows = slice(h * HEAD_DIM, (h + 1) * HEAD_DIM)
        query = cur_ref[rows, :]
        near = jnp.dot(key_ref[0, :, rows], query, preferred_element_type=jnp.float32)
        far = jnp.dot(key_ref[1, :, rows], query, preferred_element_type=jnp.float32)
        grown = jnp.exp(jnp.where(left, near, far) * scale[0:1])
        weight = (grown * (1.0 / jnp.sum(grown, axis=0, keepdims=True))).astype(jnp.bfloat16)
        near = jnp.dot(value_ref[0, rows, :], weight, preferred_element_type=jnp.float32)
        far = jnp.dot(value_ref[1, rows, :], weight, preferred_element_type=jnp.float32)
        made = (query.astype(jnp.float32) + jnp.where(left, near, far)).astype(jnp.bfloat16)
        wide = made.astype(jnp.float32)
        squares = squares + jnp.sum(wide * wide, axis=0, keepdims=True)
        if last:
            outs[0][0:ACTIVE, rows] = wide.T.astype(jnp.bfloat16)
        else:
            outs[0][rows, :] = made
    own_head = (
        lax.broadcasted_iota(jnp.int32, (512, ACTIVE), 0) // HEAD_DIM
        == lax.broadcasted_iota(jnp.int32, (512, ACTIVE), 1)
    )
    single = one_ref[...].astype(jnp.float32)
    query = jnp.where(own_head, single, 0.0).astype(jnp.bfloat16)
    scores = jnp.dot(key_ref[2], query, preferred_element_type=jnp.float32)
    grown = jnp.exp(scores * scale[1:2])
    weight = (grown * (1.0 / jnp.sum(grown, axis=0, keepdims=True))).astype(jnp.bfloat16)
    mixed = jnp.dot(value_ref[2], weight, preferred_element_type=jnp.float32)
    mixed = jnp.sum(jnp.where(own_head, mixed, 0.0), axis=1, keepdims=True)
    made = (single + mixed).astype(jnp.bfloat16)
    wide = made.astype(jnp.float32)
    if last:
        outs[0][ACTIVE : ACTIVE + 16, :] = wide.T[0:16].astype(jnp.bfloat16)
    else:
        outs[1][...] = made
        outs[2][0:1, :] = squares
        outs[2][1:2, :] = jnp.sum(wide * wide, axis=0, keepdims=True)


def run_layer(current, single, sums, keys, values, last):
    vmem = pl.BlockSpec(memory_space=pltpu.VMEM)
    if last:
        out_shape = (jax.ShapeDtypeStruct((ACTIVE + 16, 512), jnp.bfloat16),)
    else:
        out_shape = (
            jax.ShapeDtypeStruct((512, ACTIVE), jnp.bfloat16),
            jax.ShapeDtypeStruct((512, ACTIVE), jnp.bfloat16),
            jax.ShapeDtypeStruct((2, ACTIVE), jnp.float32),
        )
    return pl.pallas_call(
        functools.partial(layer_kernel, last=last),
        out_shape=out_shape,
        in_specs=[vmem] * 8,
        out_specs=(vmem,) * len(out_shape),
        compiler_params=pltpu.CompilerParams(vmem_limit_bytes=24 << 20),
        cost_estimate=pl.CostEstimate(
            flops=2 * 20 * 256 * 128 * 128, bytes_accessed=2 << 20, transcendentals=5 * 256 * 128
        ),
        name="layer",
    )(current, single, *sums, keys, values)


def rms_scale(values):
    return values * lax.rsqrt(jnp.mean(values * values, axis=-1, keepdims=True) + EPSILON)


def pick(mask, first, second):
    return jnp.where(mask.reshape(mask.shape + (1, 1)), first, second)


def fetch_encodings(pool_states, ids, place):
    xh, z, c, yh = place["xh"], place["z"], place["c"], place["yh"]
    ids_x = swapped(ids, "xh")
    ids_c = swapped(ids, "c")
    ids_xc = swapped(ids_x, "c")
    held = ring_gather(pool_states, z).reshape(64, 16, 512)
    mine = jnp.concatenate([ids, ids_x])
    theirs = jnp.concatenate([ids_c, ids_xc])

    def local(wanted):
        return ((wanted >> 4) & 7) * 8 + (wanted & 7)

    sent = jnp.take(held, local(theirs), axis=0, mode="clip")
    kept = jnp.take(held, local(mine), axis=0, mode="clip")
    got = swapped(sent, "c")
    both = pick(((mine >> 3) & 1) == c, kept, got)
    got = swapped(both[12:], "xh")
    entries = pick((ids >> 7) == xh, both[:12], got)
    entries = rms_scale(entries.astype(jnp.float32)).astype(jnp.bfloat16).reshape(2, 6, 16, 512)
    own = lax.dynamic_index_in_dim(entries, yh, 0, keepdims=False)
    got = swapped(lax.dynamic_index_in_dim(entries, 1 - yh, 0, keepdims=False), "yh")
    block = jnp.stack([own, got])
    return jnp.stack([block] + quad(block))


def spread_weights(key_weight, value_weight, query_gain):
    keys = (key_weight[0].astype(jnp.float32) * query_gain[0]).astype(jnp.bfloat16)
    joined = jnp.stack([keys, value_weight[0]])
    parts = joined.reshape(2, 16, 2, 4, SLICE).transpose(3, 0, 1, 2, 4).reshape(4, 2, 16, 2 * SLICE)
    parts = jnp.concatenate([parts, parts])
    return lax.all_to_all(parts, SECTION, 0, 0)


def per_device(
    hidden, pool_states, neighbour_ids, batch_order, key_weight, value_weight, query_gain
):
    place = {axis: lax.axis_index(axis) for axis in AXES}
    yh, yl, xl, xh, z, c = (place[axis] for axis in AXES)

    rows = spread_weights(key_weight, value_weight, query_gain)
    ids = jnp.take(neighbour_ids[:, 0], batch_order, axis=0, mode="clip").reshape(12)
    encoded = fetch_encodings(pool_states, ids, place)

    other = swapped(rows, "xh")
    is_low = xh == 0
    rows = jnp.stack([jnp.where(is_low, rows, other), jnp.where(is_low, other, rows)], axis=2)
    early = ring_gather(rows[:EARLY], z)
    late = lax.all_gather(rows[EARLY:], "z", axis=0)
    early_other = swapped(early, "c")
    late_other = swapped(late, "c")

    ordered = jnp.take(hidden[:, 0], batch_order, axis=0, mode="clip")
    start = lax.dynamic_index_in_dim(ordered, yh, 0, keepdims=False)[FIRST:]
    wide = start.astype(jnp.float32)
    total = jnp.sum(wide * wide, axis=-1)
    sums = jnp.stack([total[:ACTIVE], jnp.broadcast_to(total[ACTIVE:], (ACTIVE,))])
    nothing = jnp.zeros_like(sums)
    sums = [sums, nothing, nothing, nothing]
    mine = lax.dynamic_index_in_dim(
        start.reshape(ACTIVE + 1, 2, 4, SLICE), yl * 2 + xl, 2, keepdims=False
    ).reshape(ACTIVE + 1, 512)
    current = mine[:ACTIVE].T
    single = jnp.broadcast_to(mine[ACTIVE][:, None], (512, ACTIVE))

    core = c.reshape(1).astype(jnp.int32)
    for layer in range(LAYERS):
        last = layer == LAYERS - 1
        if layer < EARLY:
            keys, values = make_kv(core, encoded, early, early_other, layer)
        else:
            keys, values = make_kv(core, encoded, late, late_other, layer - EARLY)
        outs = run_layer(current, single, sums, keys, values, last)
        if not last:
            current, single, partial = outs
            sums = [partial] + quad(partial)
    finished = outs[0].reshape(ACTIVE + 16, 2, SLICE)
    kept = lax.dynamic_index_in_dim(finished, yh, 1, keepdims=False)
    got = swapped(lax.dynamic_index_in_dim(finished, 1 - yh, 1, keepdims=False), "yh")
    low = yh == 0
    tails = jnp.stack([jnp.where(low, kept, got), jnp.where(low, got, kept)])[:, : ACTIVE + 1]
    heads = lax.dynamic_slice_in_dim(ordered[:, :FIRST], (yh * 4 + yl * 2 + xl) * SLICE, SLICE, 2)
    return jnp.concatenate([heads, tails], axis=1)[:, None]


def solution(mesh):
    split = Mesh(mesh.devices.reshape(SIZES), AXES)
    in_specs = (
        P(None, FSDP, None, None),
        P(FSDP, SECTION, None),
        P(None, FSDP, None, None),
        P(),
        P(SECTION, FSDP, None),
        P(SECTION, FSDP, None),
        P(SECTION, None),
    )
    out_specs = P(None, FSDP, None, SECTION)
    return jax.shard_map(
        per_device, mesh=split, in_specs=in_specs, out_specs=out_specs, check_vma=False
    )
```

```python
import functools

import jax
import jax.numpy as jnp
from jax import lax
from jax.experimental import pallas as pl
from jax.experimental.pallas import tpu as pltpu
from jax.sharding import Mesh
from jax.sharding import PartitionSpec as P

HEAD_DIM = 128
SPAN_LEN = 64
LAYERS = 8
FEATURES = 2048
SLICE = 256
ACTIVE = 128
EPSILON = 1e-06
FIRST = SPAN_LEN - 1
EARLY = 5

AXES = ("yh", "yl", "xl", "xh", "z", "c")
SIZES = (2, 2, 2, 2, 8, 2)
SECTION = ("yh", "yl", "xl")
FSDP = ("xh", "z", "c")
SWAP = [(0, 1), (1, 0)]


def swapped(block, axis):
    return lax.ppermute(block, axis, SWAP)


def shifted(block, axis, size, distance):
    return lax.ppermute(block, axis, [(i, (i + distance) % size) for i in range(size)])


def gather(block):
    gathered = lax.all_gather(block.reshape(-1, 512), ("z", "c"), axis=0)
    return gathered.reshape((16,) + block.shape)


def quad(block):
    axis = ("yl", "xl")
    return [lax.ppermute(block, axis, [(i, i ^ d) for i in range(4)]) for d in (1, 2, 3)]


def after(*groups):
    return lax.optimization_barrier(groups)


def kv_kernel(enc_ref, rows_ref, key_ref, value_ref, held, sems, *, layer):
    copies = [
        pltpu.make_async_copy(
            rows_ref.at[4 * part : 4 * part + 4, layer, kv, xh],
            held.at[kv, xh, 4 * part : 4 * part + 4],
            sems.at[kv, xh, part],
        )
        for kv in range(2)
        for xh in range(2)
        for part in range(4)
    ]
    for copy in copies:
        copy.start()
    for copy in copies[:8]:
        copy.wait()
    tokens = [enc_ref[:, :, 2 * g : 2 * g + 2].reshape(256, 512) for g in range(3)]
    keys = held[0].reshape(512, 512)
    for g in range(3):
        made = jnp.dot(tokens[g], keys, preferred_element_type=jnp.float32)
        key_ref[g] = made.astype(jnp.bfloat16)
    for copy in copies[8:]:
        copy.wait()
    values = held[1].reshape(512, 512)
    for g in range(3):
        made = lax.dot_general(
            values, tokens[g], (((0,), (1,)), ((), ())), preferred_element_type=jnp.float32
        )
        value_ref[g] = made.astype(jnp.bfloat16)


def make_kv(encoded, rows, layer):
    vmem = pl.BlockSpec(memory_space=pltpu.VMEM)
    return pl.pallas_call(
        functools.partial(kv_kernel, layer=layer),
        out_shape=(
            jax.ShapeDtypeStruct((3, 256, 512), jnp.bfloat16),
            jax.ShapeDtypeStruct((3, 512, 256), jnp.bfloat16),
        ),
        in_specs=[vmem, pl.BlockSpec(memory_space=pltpu.HBM)],
        out_specs=(vmem, vmem),
        scratch_shapes=[
            pltpu.VMEM((2, 2, 16, 16, 512), jnp.bfloat16),
            pltpu.SemaphoreType.DMA((2, 2, 4)),
        ],
        compiler_params=pltpu.CompilerParams(vmem_limit_bytes=24 << 20),
        cost_estimate=pl.CostEstimate(
            flops=2 * 768 * 512 * 1024, bytes_accessed=4 << 20, transcendentals=0
        ),
        name="kv",
    )(encoded, rows)


SPOT = (0, 1, 3, 5, 7, 6, 4, 2)


def choose_kernel(code_ref, *refs):
    blocks, outs, held = refs[:9], refs[9:11], refs[11]
    for at in range(7):
        held[8 * at : 8 * at + 8] = blocks[at][...]
    held[56:60] = blocks[7][...]
    held[60:64] = blocks[8][...]
    for which, out in enumerate(outs):

        def copy(entry, carry, which=which, out=out):
            out[entry] = held[code_ref[which, entry]]
            return carry

        lax.fori_loop(0, 24, copy, 0, unroll=4)


def choose(codes, blocks):
    shape = jax.ShapeDtypeStruct((24, 16, 512), jnp.bfloat16)
    vmem = pl.BlockSpec(memory_space=pltpu.VMEM)
    return pl.pallas_call(
        choose_kernel,
        out_shape=(shape, shape),
        in_specs=[pl.BlockSpec(memory_space=pltpu.SMEM)] + [vmem] * 9,
        out_specs=(vmem, vmem),
        scratch_shapes=[pltpu.VMEM((64, 16, 512), jnp.bfloat16)],
        compiler_params=pltpu.CompilerParams(vmem_limit_bytes=16 << 20),
        name="choose",
    )(codes, *blocks)


def layer_kernel(cur_ref, one_ref, s0_ref, s1_ref, s2_ref, s3_ref, key_ref, value_ref, *outs, last):
    heads = [slice(h * HEAD_DIM, (h + 1) * HEAD_DIM) for h in range(4)]
    queries = [cur_ref[rows, :] for rows in heads]
    own_head = (
        lax.broadcasted_iota(jnp.int32, (512, ACTIVE), 0) // HEAD_DIM
        == lax.broadcasted_iota(jnp.int32, (512, ACTIVE), 1)
    )
    single = one_ref[...].astype(jnp.float32)
    queries_one = jnp.where(own_head, single, 0.0).astype(jnp.bfloat16)
    left = lax.broadcasted_iota(jnp.int32, (1, ACTIVE), 1) < SPAN_LEN

    def dot(first, second):
        return jnp.dot(first, second, preferred_element_type=jnp.float32)

    scores = [
        jnp.where(left, dot(key_ref[0, :, rows], query), dot(key_ref[1, :, rows], query))
        for rows, query in zip(heads, queries)
    ]
    scores.append(dot(key_ref[2], queries_one))
    total = s0_ref[...] + s1_ref[...] + s2_ref[...] + s3_ref[...]
    scale = lax.rsqrt(total * (1.0 / FEATURES) + EPSILON) * HEAD_DIM ** (-0.5)
    scales = [scale[0:1]] * 4 + [scale[1:2]]
    grown = [jnp.exp(score * factor) for score, factor in zip(scores, scales)]
    weights = [
        (one * (1.0 / jnp.sum(one, axis=0, keepdims=True))).astype(jnp.bfloat16) for one in grown
    ]
    mixed = [
        jnp.where(left, dot(value_ref[0, rows, :], weight), dot(value_ref[1, rows, :], weight))
        for rows, weight in zip(heads, weights)
    ]
    mixed_one = dot(value_ref[2], weights[4])
    squares = jnp.zeros((1, ACTIVE), jnp.float32)
    for rows, query, update in zip(heads, queries, mixed):
        made = (query.astype(jnp.float32) + update).astype(jnp.bfloat16)
        wide = made.astype(jnp.float32)
        squares = squares + jnp.sum(wide * wide, axis=0, keepdims=True)
        if last:
            outs[0][0:ACTIVE, rows] = wide.T.astype(jnp.bfloat16)
        else:
            outs[0][rows, :] = made
    mixed_one = jnp.sum(jnp.where(own_head, mixed_one, 0.0), axis=1, keepdims=True)
    made = (single + mixed_one).astype(jnp.bfloat16)
    wide = made.astype(jnp.float32)
    if last:
        outs[0][ACTIVE : ACTIVE + 16, :] = wide.T[0:16].astype(jnp.bfloat16)
    else:
        outs[1][...] = made
        outs[2][0:1, :] = squares
        outs[2][1:2, :] = jnp.sum(wide * wide, axis=0, keepdims=True)


def run_layer(current, single, sums, keys, values, last):
    vmem = pl.BlockSpec(memory_space=pltpu.VMEM)
    if last:
        out_shape = [jax.ShapeDtypeStruct((ACTIVE + 16, 512), jnp.bfloat16)]
    else:
        out_shape = [
            jax.ShapeDtypeStruct((512, ACTIVE), jnp.bfloat16),
            jax.ShapeDtypeStruct((512, ACTIVE), jnp.bfloat16),
            jax.ShapeDtypeStruct((2, ACTIVE), jnp.float32),
        ]
    return pl.pallas_call(
        functools.partial(layer_kernel, last=last),
        out_shape=out_shape,
        in_specs=[vmem] * 8,
        out_specs=[vmem] * len(out_shape),
        compiler_params=pltpu.CompilerParams(vmem_limit_bytes=24 << 20),
        cost_estimate=pl.CostEstimate(
            flops=2 * 20 * 256 * 128 * 128, bytes_accessed=2 << 20, transcendentals=5 * 256 * 128
        ),
        name="layer",
    )(current, single, *sums, keys, values)


def rms_scale(values):
    return values * lax.rsqrt(jnp.mean(values * values, axis=-1, keepdims=True) + EPSILON)


def pick(mask, first, second):
    return jnp.where(mask.reshape(mask.shape + (1, 1)), first, second)


def parts_kernel(key_ref, value_ref, gain_ref, out_ref):
    for q in range(4):
        for half in range(2):
            spot = 4 * half + q
            source = slice(spot * SLICE, (spot + 1) * SLICE)
            target = slice(half * SLICE, (half + 1) * SLICE)
            keys = key_ref[0, :, source].astype(jnp.float32) * gain_ref[:, source]
            for yh in range(2):
                out_ref[4 * yh + q, 0, :, target] = keys.astype(jnp.bfloat16)
                out_ref[4 * yh + q, 1, :, target] = value_ref[0, :, source]


def weight_parts(key_weight, value_weight, query_gain):
    vmem = pl.BlockSpec(memory_space=pltpu.VMEM)
    return pl.pallas_call(
        parts_kernel,
        out_shape=jax.ShapeDtypeStruct((8, 2, 16, 512), jnp.bfloat16),
        in_specs=[vmem] * 3,
        out_specs=vmem,
        name="parts",
    )(key_weight, value_weight, query_gain)


def per_device(
    hidden, pool_states, neighbour_ids, batch_order, key_weight, value_weight, query_gain
):
    place = {axis: lax.axis_index(axis) for axis in AXES}
    yh, yl, xl, xh, z, c = (place[axis] for axis in AXES)

    is_low = xh == 0

    def both_halves(part, other):
        halves = [jnp.where(is_low, part, other), jnp.where(is_low, other, part)]
        return jnp.stack(halves, axis=2)

    def up(block):
        return shifted(block, "z", 8, 1)

    def down(block):
        return shifted(block, "z", 8, -1)

    parts = weight_parts(key_weight, value_weight, query_gain)
    parts, neighbour_ids = after(parts, neighbour_ids)
    rows = lax.all_to_all(parts, SECTION, 0, 0)
    ids = jnp.take(neighbour_ids[:, 0], batch_order, axis=0, mode="clip").reshape(2, 6)
    own = lax.dynamic_index_in_dim(ids, yh, 0, keepdims=False)
    ids = jnp.concatenate([own, lax.dynamic_index_in_dim(ids, 1 - yh, 0, keepdims=False)])
    ids, pool_states = after(ids, pool_states)
    up_1, down_1 = up(pool_states), down(pool_states)
    up_1, down_1, ids, rows = after(up_1, down_1, ids, rows)

    up_2, down_2 = up(up_1), down(down_1)
    block = both_halves(rows[:EARLY], swapped(rows[:EARLY], "xh"))
    pair = jnp.stack([ids, swapped(ids, "c")])
    up_2, down_2, pair, block, rows = after(up_2, down_2, pair, block, rows)

    up_3, down_3 = up(up_2), down(down_2)
    late = both_halves(rows[EARLY:], swapped(rows[EARLY:], "xh"))
    theirs = jnp.concatenate([pair, swapped(pair, "xh")], axis=1)
    codes = jnp.asarray(SPOT, jnp.int32)[(z - (theirs >> 4)) & 7] * 8 + (theirs & 7)
    up_3, down_3, late, codes = after(up_3, down_3, late, codes)

    early = gather(block)
    opposite = [up(up_3[:4]), down(down_3[4:])]
    pool = [pool_states, up_1, down_1, up_2, down_2, up_3, down_3] + opposite
    kept, sent = choose(codes, pool)
    both = pick(((theirs[0] >> 3) & 1) == c, kept, swapped(sent, "c")).reshape(4, 6, 16, 512)

    from_y, from_x, from_xy = after(
        *(
            lax.ppermute(both[part], ("yh", "xh"), [(i, i ^ d) for i in range(4)])
            for part, d in ((1, 2), (2, 1), (3, 3))
        )
    )
    here = (own >> 7) == xh
    tokens = jnp.stack([pick(here, both[0], from_x), pick(here, from_y, from_xy)])
    tokens = rms_scale(tokens.astype(jnp.float32)).astype(jnp.bfloat16)

    tokens, hidden = after(tokens, hidden)
    encoded = jnp.stack([tokens] + quad(tokens))
    ordered = jnp.take(hidden[:, 0], batch_order, axis=0, mode="clip")
    start = lax.dynamic_index_in_dim(ordered, yh, 0, keepdims=False)[FIRST:]
    wide = start.astype(jnp.float32)
    total = jnp.sum(wide * wide, axis=-1)
    sums = jnp.stack([total[:ACTIVE], jnp.broadcast_to(total[ACTIVE:], (ACTIVE,))])
    mine = jnp.concatenate(
        [
            lax.dynamic_slice_in_dim(start, (4 * half + yl * 2 + xl) * SLICE, SLICE, 1)
            for half in range(2)
        ],
        axis=1,
    )
    current = mine[:ACTIVE].T
    single = jnp.broadcast_to(mine[ACTIVE][:, None], (512, ACTIVE))
    encoded, sums, current, single = after(encoded, sums, current, single)

    nothing = jnp.zeros_like(sums)
    sums = [sums, nothing, nothing, nothing]
    late = gather(late)
    for layer in range(LAYERS):
        last = layer == LAYERS - 1
        if layer < EARLY:
            keys, values = make_kv(encoded, early, layer)
        else:
            keys, values = make_kv(encoded, late, layer - EARLY)
        outs = run_layer(current, single, sums, keys, values, last)
        if not last:
            current, single, partial = outs
            sums = [partial] + quad(partial)
    finished = outs[0].reshape(ACTIVE + 16, 2, SLICE)
    kept = lax.dynamic_index_in_dim(finished, yh, 1, keepdims=False)
    got = swapped(lax.dynamic_index_in_dim(finished, 1 - yh, 1, keepdims=False), "yh")
    low = yh == 0
    tails = jnp.stack([jnp.where(low, kept, got), jnp.where(low, got, kept)])[:, : ACTIVE + 1]
    heads = lax.dynamic_slice_in_dim(ordered[:, :FIRST], (yh * 4 + yl * 2 + xl) * SLICE, SLICE, 2)
    return jnp.concatenate([heads, tails], axis=1)[:, None]


def solution(mesh):
    split = Mesh(mesh.devices.reshape(SIZES), AXES)
    in_specs = (
        P(None, FSDP, None, None),
        P(FSDP, SECTION, None),
        P(None, FSDP, None, None),
        P(),
        P(SECTION, FSDP, None),
        P(SECTION, FSDP, None),
        P(SECTION, None),
    )
    out_specs = P(None, FSDP, None, SECTION)
    return jax.shard_map(
        per_device, mesh=split, in_specs=in_specs, out_specs=out_specs, check_vma=False
    )
```

```python
import functools

import jax
import jax.numpy as jnp
from jax import lax
from jax.experimental import pallas as pl
from jax.experimental.pallas import tpu as pltpu
from jax.sharding import Mesh
from jax.sharding import PartitionSpec as P

HEAD_DIM = 128
SPAN_LEN = 64
LAYERS = 8
FEATURES = 2048
SLICE = 256
ACTIVE = 128
EPSILON = 1e-06
FIRST = SPAN_LEN - 1
EARLY = 6

AXES = ("yh", "yl", "xl", "xh", "z", "c")
SIZES = (2, 2, 2, 2, 8, 2)
SECTION = ("yh", "yl", "xl")
FSDP = ("xh", "z", "c")
SWAP = [(0, 1), (1, 0)]


def swapped(block, axis):
    return lax.ppermute(block, axis, SWAP)


def shifted(block, axis, size, distance):
    return lax.ppermute(block, axis, [(i, (i + distance) % size) for i in range(size)])


def gather(block):
    gathered = lax.all_gather(block.reshape(-1, 512), ("z", "c"), axis=0)
    return gathered.reshape((16,) + block.shape)


def flipped(block, axes):
    last = 4 ** (len(axes) // 2) - 1
    return lax.ppermute(block, axes, [(i, last - i) for i in range(last + 1)])


FLIP_Y = ("yh", "yl")
FLIP_X = ("xl", "xh")


def quad(block):
    axis = ("yl", "xl")
    return [lax.ppermute(block, axis, [(i, i ^ d) for i in range(4)]) for d in (1, 2, 3)]


def after(*groups):
    return lax.optimization_barrier(groups)


def kv_kernel(enc_ref, rows_ref, key_ref, value_ref, held, sems, *, layer):
    copies = [
        pltpu.make_async_copy(
            rows_ref.at[4 * part : 4 * part + 4, layer, kv, xh],
            held.at[kv, xh, 4 * part : 4 * part + 4],
            sems.at[kv, xh, part],
        )
        for kv in range(2)
        for xh in range(2)
        for part in range(4)
    ]
    for copy in copies:
        copy.start()
    for copy in copies[:8]:
        copy.wait()
    tokens = [enc_ref[:, :, 2 * g : 2 * g + 2].reshape(256, 512) for g in range(3)]
    keys = held[0].reshape(512, 512)
    for g in range(3):
        made = jnp.dot(tokens[g], keys, preferred_element_type=jnp.float32)
        key_ref[g] = made.astype(jnp.bfloat16)
    for copy in copies[8:]:
        copy.wait()
    values = held[1].reshape(512, 512)
    for g in range(3):
        made = lax.dot_general(
            values, tokens[g], (((0,), (1,)), ((), ())), preferred_element_type=jnp.float32
        )
        value_ref[g] = made.astype(jnp.bfloat16)


def make_kv(encoded, rows, layer):
    vmem = pl.BlockSpec(memory_space=pltpu.VMEM)
    return pl.pallas_call(
        functools.partial(kv_kernel, layer=layer),
        out_shape=(
            jax.ShapeDtypeStruct((3, 256, 512), jnp.bfloat16),
            jax.ShapeDtypeStruct((3, 512, 256), jnp.bfloat16),
        ),
        in_specs=[vmem, pl.BlockSpec(memory_space=pltpu.HBM)],
        out_specs=(vmem, vmem),
        scratch_shapes=[
            pltpu.VMEM((2, 2, 16, 16, 512), jnp.bfloat16),
            pltpu.SemaphoreType.DMA((2, 2, 4)),
        ],
        compiler_params=pltpu.CompilerParams(vmem_limit_bytes=24 << 20),
        cost_estimate=pl.CostEstimate(
            flops=2 * 768 * 512 * 1024, bytes_accessed=4 << 20, transcendentals=0
        ),
        name="kv",
    )(encoded, pltpu.with_memory_space_constraint(rows, pltpu.HBM))


SPOT = (0, 1, 3, 5, 7, 6, 4, 2)


def choose_kernel(code_ref, *refs):
    blocks, outs, held = refs[:8], refs[8:10], refs[10]
    for at in range(8):
        held[8 * at : 8 * at + 8] = blocks[at][...]
    for which, out in enumerate(outs):

        def copy(entry, carry, which=which, out=out):
            out[entry] = held[code_ref[which, entry]]
            return carry

        lax.fori_loop(0, 24, copy, 0, unroll=4)


def choose(codes, blocks):
    shape = jax.ShapeDtypeStruct((24, 16, 512), jnp.bfloat16)
    vmem = pl.BlockSpec(memory_space=pltpu.VMEM)
    return pl.pallas_call(
        choose_kernel,
        out_shape=(shape, shape),
        in_specs=[pl.BlockSpec(memory_space=pltpu.SMEM)] + [vmem] * 8,
        out_specs=(vmem, vmem),
        scratch_shapes=[pltpu.VMEM((64, 16, 512), jnp.bfloat16)],
        compiler_params=pltpu.CompilerParams(vmem_limit_bytes=16 << 20),
        name="choose",
    )(codes, *blocks)


def layer_kernel(cur_ref, one_ref, s0_ref, s1_ref, s2_ref, s3_ref, key_ref, value_ref, *outs, last):
    heads = [slice(h * HEAD_DIM, (h + 1) * HEAD_DIM) for h in range(4)]
    queries = [cur_ref[rows, :] for rows in heads]
    own_head = (
        lax.broadcasted_iota(jnp.int32, (512, ACTIVE), 0) // HEAD_DIM
        == lax.broadcasted_iota(jnp.int32, (512, ACTIVE), 1)
    )
    single = one_ref[...].astype(jnp.float32)
    queries_one = jnp.where(own_head, single, 0.0).astype(jnp.bfloat16)
    left = lax.broadcasted_iota(jnp.int32, (1, ACTIVE), 1) < SPAN_LEN

    def dot(first, second):
        return jnp.dot(first, second, preferred_element_type=jnp.float32)

    scores = [
        jnp.where(left, dot(key_ref[0, :, rows], query), dot(key_ref[1, :, rows], query))
        for rows, query in zip(heads, queries)
    ]
    scores.append(dot(key_ref[2], queries_one))
    total = s0_ref[...] + s1_ref[...] + s2_ref[...] + s3_ref[...]
    scale = lax.rsqrt(total * (1.0 / FEATURES) + EPSILON) * HEAD_DIM ** (-0.5)
    scales = [scale[0:1]] * 4 + [scale[1:2]]
    grown = [jnp.exp(score * factor) for score, factor in zip(scores, scales)]
    weights = [
        (one * (1.0 / jnp.sum(one, axis=0, keepdims=True))).astype(jnp.bfloat16) for one in grown
    ]
    mixed = [
        jnp.where(left, dot(value_ref[0, rows, :], weight), dot(value_ref[1, rows, :], weight))
        for rows, weight in zip(heads, weights)
    ]
    mixed_one = dot(value_ref[2], weights[4])
    squares = jnp.zeros((1, ACTIVE), jnp.float32)
    for rows, query, update in zip(heads, queries, mixed):
        made = (query.astype(jnp.float32) + update).astype(jnp.bfloat16)
        wide = made.astype(jnp.float32)
        squares = squares + jnp.sum(wide * wide, axis=0, keepdims=True)
        if last:
            outs[0][0:ACTIVE, rows] = wide.T.astype(jnp.bfloat16)
        else:
            outs[0][rows, :] = made
    mixed_one = jnp.sum(jnp.where(own_head, mixed_one, 0.0), axis=1, keepdims=True)
    made = (single + mixed_one).astype(jnp.bfloat16)
    wide = made.astype(jnp.float32)
    if last:
        outs[0][ACTIVE : ACTIVE + 16, :] = wide.T[0:16].astype(jnp.bfloat16)
    else:
        outs[1][...] = made
        outs[2][0:1, :] = squares
        outs[2][1:2, :] = jnp.sum(wide * wide, axis=0, keepdims=True)


def run_layer(current, single, sums, keys, values, last):
    vmem = pl.BlockSpec(memory_space=pltpu.VMEM)
    if last:
        out_shape = [jax.ShapeDtypeStruct((ACTIVE + 16, 512), jnp.bfloat16)]
    else:
        out_shape = [
            jax.ShapeDtypeStruct((512, ACTIVE), jnp.bfloat16),
            jax.ShapeDtypeStruct((512, ACTIVE), jnp.bfloat16),
            jax.ShapeDtypeStruct((2, ACTIVE), jnp.float32),
        ]
    return pl.pallas_call(
        functools.partial(layer_kernel, last=last),
        out_shape=out_shape,
        in_specs=[vmem] * 8,
        out_specs=[vmem] * len(out_shape),
        compiler_params=pltpu.CompilerParams(vmem_limit_bytes=24 << 20),
        cost_estimate=pl.CostEstimate(
            flops=2 * 20 * 256 * 128 * 128, bytes_accessed=2 << 20, transcendentals=5 * 256 * 128
        ),
        name="layer",
    )(current, single, *sums, keys, values)


def rms_scale(values):
    return values * lax.rsqrt(jnp.mean(values * values, axis=-1, keepdims=True) + EPSILON)


def pick(mask, first, second):
    return jnp.where(mask.reshape(mask.shape + (1, 1)), first, second)


def parts_kernel(key_ref, value_ref, gain_ref, out_ref):
    for label in range(2):
        for xl in range(2):
            for half, y in enumerate((label, 3 - label)):
                spot = 2 * y + xl
                source = slice(spot * SLICE, (spot + 1) * SLICE)
                target = slice(half * SLICE, (half + 1) * SLICE)
                keys = key_ref[0, :, source].astype(jnp.float32) * gain_ref[:, source]
                for section in (2 * label + xl, 2 * (3 - label) + xl):
                    out_ref[section, 0, :, target] = keys.astype(jnp.bfloat16)
                    out_ref[section, 1, :, target] = value_ref[0, :, source]


def weight_parts(key_weight, value_weight, query_gain):
    vmem = pl.BlockSpec(memory_space=pltpu.VMEM)
    return pl.pallas_call(
        parts_kernel,
        out_shape=jax.ShapeDtypeStruct((8, 2, 16, 512), jnp.bfloat16),
        in_specs=[vmem] * 3,
        out_specs=vmem,
        name="parts",
    )(key_weight, value_weight, query_gain)


def per_device(
    hidden, pool_states, neighbour_ids, batch_order, key_weight, value_weight, query_gain
):
    place = {axis: lax.axis_index(axis) for axis in AXES}
    yh, yl, xl, xh, z, c = (place[axis] for axis in AXES)

    is_low = xh == 0
    label = yl ^ yh

    def both_halves(part, other):
        halves = [jnp.where(is_low, part, other), jnp.where(is_low, other, part)]
        return jnp.stack(halves, axis=2)

    def up(block):
        return shifted(block, "z", 8, 1)

    def down(block):
        return shifted(block, "z", 8, -1)

    parts = weight_parts(key_weight, value_weight, query_gain)
    parts, neighbour_ids = after(parts, neighbour_ids)
    rows = lax.all_to_all(parts, SECTION, 0, 0)
    ids = jnp.take(neighbour_ids[:, 0], batch_order, axis=0, mode="clip").reshape(2, 6)
    own = lax.dynamic_index_in_dim(ids, yh, 0, keepdims=False)
    ids = jnp.concatenate([own, lax.dynamic_index_in_dim(ids, 1 - yh, 0, keepdims=False)])
    ids, pool_states = after(ids, pool_states)
    up_1, down_1 = up(pool_states), down(pool_states)
    up_1, down_1, ids, rows = after(up_1, down_1, ids, rows)

    up_2, down_2 = up(up_1), down(down_1)
    block = both_halves(rows[:EARLY], swapped(rows[:EARLY], "xh"))
    pair = jnp.stack([ids, swapped(ids, "c")])
    opposite = shifted(pool_states, "z", 8, 4)
    up_2, down_2, pair, block, rows = after(up_2, down_2, pair, block, rows)

    up_3, down_3 = up(up_2), down(down_2)
    late = both_halves(rows[EARLY:], swapped(rows[EARLY:], "xh"))
    theirs = jnp.concatenate([pair, flipped(pair, FLIP_X)], axis=1)
    codes = jnp.asarray(SPOT, jnp.int32)[(z - (theirs >> 4)) & 7] * 8 + (theirs & 7)
    up_3, down_3, opposite, late, codes = after(up_3, down_3, opposite, late, codes)

    early = gather(block)
    pool = [pool_states, up_1, down_1, up_2, down_2, up_3, down_3, opposite]
    kept, sent = choose(codes, pool)
    both = pick(((theirs[0] >> 3) & 1) == c, kept, swapped(sent, "c")).reshape(4, 6, 16, 512)

    from_y, from_x, from_xy = after(
        *(
            flipped(both[part], axes)
            for part, axes in ((1, FLIP_Y), (2, FLIP_X), (3, FLIP_Y + FLIP_X))
        )
    )
    here = (own >> 7) == xh
    tokens = jnp.stack([pick(here, both[0], from_x), pick(here, from_y, from_xy)])
    tokens = rms_scale(tokens.astype(jnp.float32)).astype(jnp.bfloat16)

    tokens, hidden = after(tokens, hidden)
    encoded = jnp.stack([tokens] + quad(tokens))
    ordered = jnp.take(hidden[:, 0], batch_order, axis=0, mode="clip")
    start = lax.dynamic_index_in_dim(ordered, yh, 0, keepdims=False)[FIRST:]
    wide = start.astype(jnp.float32)
    total = jnp.sum(wide * wide, axis=-1)
    sums = jnp.stack([total[:ACTIVE], jnp.broadcast_to(total[ACTIVE:], (ACTIVE,))])
    mine = jnp.concatenate(
        [
            lax.dynamic_slice_in_dim(start, (2 * y + xl) * SLICE, SLICE, 1)
            for y in (label, 3 - label)
        ],
        axis=1,
    )
    current = mine[:ACTIVE].T
    single = jnp.broadcast_to(mine[ACTIVE][:, None], (512, ACTIVE))
    encoded, sums, current, single = after(encoded, sums, current, single)

    nothing = jnp.zeros_like(sums)
    sums = [sums, nothing, nothing, nothing]
    late = gather(late)
    for layer in range(LAYERS):
        last = layer == LAYERS - 1
        if layer < EARLY:
            keys, values = make_kv(encoded, early, layer)
        else:
            keys, values = make_kv(encoded, late, layer - EARLY)
        outs = run_layer(current, single, sums, keys, values, last)
        if not last:
            current, single, partial = outs
            sums = [partial] + quad(partial)
    finished = outs[0].reshape(ACTIVE + 16, 2, SLICE)
    kept = lax.dynamic_index_in_dim(finished, yh, 1, keepdims=False)
    got = flipped(lax.dynamic_index_in_dim(finished, 1 - yh, 1, keepdims=False), FLIP_Y)
    low = yh == 0
    tails = jnp.stack([jnp.where(low, kept, got), jnp.where(low, got, kept)])[:, : ACTIVE + 1]
    heads = lax.dynamic_slice_in_dim(ordered[:, :FIRST], (yh * 4 + yl * 2 + xl) * SLICE, SLICE, 2)
    return jnp.concatenate([heads, tails], axis=1)[:, None]


def solution(mesh):
    split = Mesh(mesh.devices.reshape(SIZES), AXES)
    in_specs = (
        P(None, FSDP, None, None),
        P(FSDP, SECTION, None),
        P(None, FSDP, None, None),
        P(),
        P(SECTION, FSDP, None),
        P(SECTION, FSDP, None),
        P(SECTION, None),
    )
    out_specs = P(None, FSDP, None, SECTION)
    return jax.shard_map(
        per_device, mesh=split, in_specs=in_specs, out_specs=out_specs, check_vma=False
    )
```

```python
import functools

import jax
import jax.numpy as jnp
from jax import lax
from jax.experimental import pallas as pl
from jax.experimental.pallas import tpu as pltpu
from jax.sharding import Mesh
from jax.sharding import PartitionSpec as P

HEAD_DIM = 128
SPAN_LEN = 64
LAYERS = 8
FEATURES = 2048
SLICE = 256
ACTIVE = 128
EPSILON = 1e-06
FIRST = SPAN_LEN - 1
EARLY = 6

AXES = ("yh", "yl", "xl", "xh", "z", "c")
SIZES = (2, 2, 2, 2, 8, 2)
SECTION = ("yh", "yl", "xl")
FSDP = ("xh", "z", "c")
SWAP = [(0, 1), (1, 0)]


def swapped(block, axis):
    return lax.ppermute(block, axis, SWAP)


def shifted(block, axis, size, distance):
    return lax.ppermute(block, axis, [(i, (i + distance) % size) for i in range(size)])


def gather(block):
    gathered = lax.all_gather(block.reshape(-1, 512), ("z", "c"), axis=0)
    return gathered.reshape((16,) + block.shape)


def flipped(block, axes):
    last = 4 ** (len(axes) // 2) - 1
    return lax.ppermute(block, axes, [(i, last - i) for i in range(last + 1)])


FLIP_Y = ("yh", "yl")
FLIP_X = ("xl", "xh")


def quad(block):
    axis = ("yl", "xl")
    return [lax.ppermute(block, axis, [(i, i ^ d) for i in range(4)]) for d in (1, 2, 3)]


def after(*groups):
    return lax.optimization_barrier(groups)


def kv_kernel(layer_ref, enc_ref, rows_ref, key_ref, value_ref, held, sems):
    layer = layer_ref[0]
    copies = [
        pltpu.make_async_copy(
            rows_ref.at[4 * part : 4 * part + 4, layer, kv, xh],
            held.at[kv, xh, 4 * part : 4 * part + 4],
            sems.at[kv, xh, part],
        )
        for kv in range(2)
        for xh in range(2)
        for part in range(4)
    ]
    for copy in copies:
        copy.start()
    for copy in copies[:8]:
        copy.wait()

    def tokens(g):
        return enc_ref[:, :, pl.ds(2 * g, 2)].reshape(256, 512)

    def keys(g, carry):
        made = jnp.dot(
            tokens(g), held[0].reshape(512, 512), preferred_element_type=jnp.float32
        )
        key_ref[g] = made.astype(jnp.bfloat16)
        return carry

    lax.fori_loop(0, 3, keys, 0)
    for copy in copies[8:]:
        copy.wait()

    def values(g, carry):
        made = lax.dot_general(
            held[1].reshape(512, 512),
            tokens(g),
            (((0,), (1,)), ((), ())),
            preferred_element_type=jnp.float32,
        )
        value_ref[g] = made.astype(jnp.bfloat16)
        return carry

    lax.fori_loop(0, 3, values, 0)


def make_kv(encoded, rows, layer):
    vmem = pl.BlockSpec(memory_space=pltpu.VMEM)
    return pl.pallas_call(
        kv_kernel,
        out_shape=(
            jax.ShapeDtypeStruct((3, 256, 512), jnp.bfloat16),
            jax.ShapeDtypeStruct((3, 512, 256), jnp.bfloat16),
        ),
        in_specs=[
            pl.BlockSpec(memory_space=pltpu.SMEM),
            vmem,
            pl.BlockSpec(memory_space=pltpu.HBM),
        ],
        out_specs=(vmem, vmem),
        scratch_shapes=[
            pltpu.VMEM((2, 2, 16, 16, 512), jnp.bfloat16),
            pltpu.SemaphoreType.DMA((2, 2, 4)),
        ],
        compiler_params=pltpu.CompilerParams(vmem_limit_bytes=24 << 20),
        cost_estimate=pl.CostEstimate(
            flops=2 * 768 * 512 * 1024, bytes_accessed=4 << 20, transcendentals=0
        ),
        name="kv",
    )(
        jnp.full((1,), layer, jnp.int32),
        encoded,
        pltpu.with_memory_space_constraint(rows, pltpu.HBM),
    )


SPOT = (0, 1, 3, 5, 7, 6, 4, 2)


def choose_kernel(code_ref, *refs):
    blocks, outs, held = refs[:8], refs[8:10], refs[10]
    for at in range(8):
        held[8 * at : 8 * at + 8] = blocks[at][...]
    for which, out in enumerate(outs):

        def copy(entry, carry, which=which, out=out):
            out[entry] = held[code_ref[which, entry]]
            return carry

        lax.fori_loop(0, 24, copy, 0, unroll=4)


def choose(codes, blocks):
    shape = jax.ShapeDtypeStruct((24, 16, 512), jnp.bfloat16)
    vmem = pl.BlockSpec(memory_space=pltpu.VMEM)
    return pl.pallas_call(
        choose_kernel,
        out_shape=(shape, shape),
        in_specs=[pl.BlockSpec(memory_space=pltpu.SMEM)] + [vmem] * 8,
        out_specs=(vmem, vmem),
        scratch_shapes=[pltpu.VMEM((64, 16, 512), jnp.bfloat16)],
        compiler_params=pltpu.CompilerParams(vmem_limit_bytes=16 << 20),
        name="choose",
    )(codes, *blocks)


def layer_kernel(cur_ref, one_ref, s0_ref, s1_ref, s2_ref, s3_ref, key_ref, value_ref, *outs, last):
    heads = [slice(h * HEAD_DIM, (h + 1) * HEAD_DIM) for h in range(4)]
    queries = [cur_ref[rows, :] for rows in heads]
    own_head = (
        lax.broadcasted_iota(jnp.int32, (512, ACTIVE), 0) // HEAD_DIM
        == lax.broadcasted_iota(jnp.int32, (512, ACTIVE), 1)
    )
    single = one_ref[...].astype(jnp.float32)
    queries_one = jnp.where(own_head, single, 0.0).astype(jnp.bfloat16)
    left = lax.broadcasted_iota(jnp.int32, (1, ACTIVE), 1) < SPAN_LEN

    def dot(first, second):
        return jnp.dot(first, second, preferred_element_type=jnp.float32)

    scores = [
        jnp.where(left, dot(key_ref[0, :, rows], query), dot(key_ref[1, :, rows], query))
        for rows, query in zip(heads, queries)
    ]
    scores.append(dot(key_ref[2], queries_one))
    total = s0_ref[...] + s1_ref[...] + s2_ref[...] + s3_ref[...]
    scale = lax.rsqrt(total * (1.0 / FEATURES) + EPSILON) * HEAD_DIM ** (-0.5)
    scales = [scale[0:1]] * 4 + [scale[1:2]]
    grown = [jnp.exp(score * factor) for score, factor in zip(scores, scales)]
    weights = [
        (one * (1.0 / jnp.sum(one, axis=0, keepdims=True))).astype(jnp.bfloat16) for one in grown
    ]
    mixed = [
        jnp.where(left, dot(value_ref[0, rows, :], weight), dot(value_ref[1, rows, :], weight))
        for rows, weight in zip(heads, weights)
    ]
    mixed_one = dot(value_ref[2], weights[4])
    squares = jnp.zeros((1, ACTIVE), jnp.float32)
    for rows, query, update in zip(heads, queries, mixed):
        made = (query.astype(jnp.float32) + update).astype(jnp.bfloat16)
        wide = made.astype(jnp.float32)
        squares = squares + jnp.sum(wide * wide, axis=0, keepdims=True)
        if last:
            outs[0][0:ACTIVE, rows] = wide.T.astype(jnp.bfloat16)
        else:
            outs[0][rows, :] = made
    mixed_one = jnp.sum(jnp.where(own_head, mixed_one, 0.0), axis=1, keepdims=True)
    made = (single + mixed_one).astype(jnp.bfloat16)
    wide = made.astype(jnp.float32)
    if last:
        outs[0][ACTIVE : ACTIVE + 16, :] = wide.T[0:16].astype(jnp.bfloat16)
    else:
        outs[1][...] = made
        outs[2][0:1, :] = squares
        outs[2][1:2, :] = jnp.sum(wide * wide, axis=0, keepdims=True)


def run_layer(current, single, sums, keys, values, last):
    vmem = pl.BlockSpec(memory_space=pltpu.VMEM)
    if last:
        out_shape = [jax.ShapeDtypeStruct((ACTIVE + 16, 512), jnp.bfloat16)]
    else:
        out_shape = [
            jax.ShapeDtypeStruct((512, ACTIVE), jnp.bfloat16),
            jax.ShapeDtypeStruct((512, ACTIVE), jnp.bfloat16),
            jax.ShapeDtypeStruct((2, ACTIVE), jnp.float32),
        ]
    return pl.pallas_call(
        functools.partial(layer_kernel, last=last),
        out_shape=out_shape,
        in_specs=[vmem] * 8,
        out_specs=[vmem] * len(out_shape),
        compiler_params=pltpu.CompilerParams(vmem_limit_bytes=24 << 20),
        cost_estimate=pl.CostEstimate(
            flops=2 * 20 * 256 * 128 * 128, bytes_accessed=2 << 20, transcendentals=5 * 256 * 128
        ),
        name="layer",
    )(current, single, *sums, keys, values)


def rms_scale(values):
    return values * lax.rsqrt(jnp.mean(values * values, axis=-1, keepdims=True) + EPSILON)


def pick(mask, first, second):
    return jnp.where(mask.reshape(mask.shape + (1, 1)), first, second)


def parts_kernel(key_ref, value_ref, gain_ref, out_ref):
    for label in range(2):
        for xl in range(2):
            for half, y in enumerate((label, 3 - label)):
                spot = 2 * y + xl
                source = slice(spot * SLICE, (spot + 1) * SLICE)
                target = slice(half * SLICE, (half + 1) * SLICE)
                keys = key_ref[0, :, source].astype(jnp.float32) * gain_ref[:, source]
                for section in (2 * label + xl, 2 * (3 - label) + xl):
                    out_ref[section, 0, :, target] = keys.astype(jnp.bfloat16)
                    out_ref[section, 1, :, target] = value_ref[0, :, source]


def weight_parts(key_weight, value_weight, query_gain):
    vmem = pl.BlockSpec(memory_space=pltpu.VMEM)
    return pl.pallas_call(
        parts_kernel,
        out_shape=jax.ShapeDtypeStruct((8, 2, 16, 512), jnp.bfloat16),
        in_specs=[vmem] * 3,
        out_specs=vmem,
        name="parts",
    )(key_weight, value_weight, query_gain)


def per_device(
    hidden, pool_states, neighbour_ids, batch_order, key_weight, value_weight, query_gain
):
    place = {axis: lax.axis_index(axis) for axis in AXES}
    yh, yl, xl, xh, z, c = (place[axis] for axis in AXES)

    is_low = xh == 0
    label = yl ^ yh

    def both_halves(part, other):
        halves = [jnp.where(is_low, part, other), jnp.where(is_low, other, part)]
        return jnp.stack(halves, axis=2)

    def up(block):
        return shifted(block, "z", 8, 1)

    def down(block):
        return shifted(block, "z", 8, -1)

    parts = weight_parts(key_weight, value_weight, query_gain)
    parts, neighbour_ids = after(parts, neighbour_ids)
    rows = lax.all_to_all(parts, SECTION, 0, 0)
    ids = jnp.take(neighbour_ids[:, 0], batch_order, axis=0, mode="clip").reshape(2, 6)
    own = lax.dynamic_index_in_dim(ids, yh, 0, keepdims=False)
    ids = jnp.concatenate([own, lax.dynamic_index_in_dim(ids, 1 - yh, 0, keepdims=False)])
    ids, pool_states = after(ids, pool_states)
    up_1, down_1 = up(pool_states), down(pool_states)
    up_1, down_1, ids, rows = after(up_1, down_1, ids, rows)

    up_2, down_2 = up(up_1), down(down_1)
    rows = both_halves(rows, swapped(rows, "xh"))
    pair = jnp.stack([ids, swapped(ids, "c")])
    opposite = shifted(pool_states, "z", 8, 4)
    up_2, down_2, pair, rows = after(up_2, down_2, pair, rows)
    block, late = rows[:EARLY], rows[EARLY:]

    up_3, down_3 = up(up_2), down(down_2)
    theirs = jnp.concatenate([pair, flipped(pair, FLIP_X)], axis=1)
    codes = jnp.asarray(SPOT, jnp.int32)[(z - (theirs >> 4)) & 7] * 8 + (theirs & 7)
    up_3, down_3, opposite, codes = after(up_3, down_3, opposite, codes)

    early = gather(block)
    pool = [pool_states, up_1, down_1, up_2, down_2, up_3, down_3, opposite]
    kept, sent = choose(codes, pool)
    both = pick(((theirs[0] >> 3) & 1) == c, kept, swapped(sent, "c")).reshape(4, 6, 16, 512)

    from_y, from_x, from_xy = after(
        *(
            flipped(both[part], axes)
            for part, axes in ((1, FLIP_Y), (2, FLIP_X), (3, FLIP_Y + FLIP_X))
        )
    )
    here = (own >> 7) == xh
    tokens = jnp.stack([pick(here, both[0], from_x), pick(here, from_y, from_xy)])
    tokens = rms_scale(tokens.astype(jnp.float32)).astype(jnp.bfloat16)

    tokens, hidden = after(tokens, hidden)
    encoded = jnp.stack([tokens] + quad(tokens))
    ordered = jnp.take(hidden[:, 0], batch_order, axis=0, mode="clip")
    start = lax.dynamic_index_in_dim(ordered, yh, 0, keepdims=False)[FIRST:]
    wide = start.astype(jnp.float32)
    total = jnp.sum(wide * wide, axis=-1)
    sums = jnp.stack([total[:ACTIVE], jnp.broadcast_to(total[ACTIVE:], (ACTIVE,))])
    mine = jnp.concatenate(
        [
            lax.dynamic_slice_in_dim(start, (2 * y + xl) * SLICE, SLICE, 1)
            for y in (label, 3 - label)
        ],
        axis=1,
    )
    current = mine[:ACTIVE].T
    single = jnp.broadcast_to(mine[ACTIVE][:, None], (512, ACTIVE))
    encoded, sums, current, single = after(encoded, sums, current, single)

    nothing = jnp.zeros_like(sums)
    sums = [sums, nothing, nothing, nothing]
    late = gather(late)
    for layer in range(LAYERS):
        last = layer == LAYERS - 1
        if layer < EARLY:
            keys, values = make_kv(encoded, early, layer)
        else:
            keys, values = make_kv(encoded, late, layer - EARLY)
        outs = run_layer(current, single, sums, keys, values, last)
        if not last:
            current, single, partial = outs
            sums = [partial] + quad(partial)
    finished = outs[0].reshape(ACTIVE + 16, 2, SLICE)
    kept = lax.dynamic_index_in_dim(finished, yh, 1, keepdims=False)
    got = flipped(lax.dynamic_index_in_dim(finished, 1 - yh, 1, keepdims=False), FLIP_Y)
    low = yh == 0
    tails = jnp.stack([jnp.where(low, kept, got), jnp.where(low, got, kept)])[:, : ACTIVE + 1]
    heads = lax.dynamic_slice_in_dim(ordered[:, :FIRST], (yh * 4 + yl * 2 + xl) * SLICE, SLICE, 2)
    return jnp.concatenate([heads, tails], axis=1)[:, None]


def solution(mesh):
    split = Mesh(mesh.devices.reshape(SIZES), AXES)
    in_specs = (
        P(None, FSDP, None, None),
        P(FSDP, SECTION, None),
        P(None, FSDP, None, None),
        P(),
        P(SECTION, FSDP, None),
        P(SECTION, FSDP, None),
        P(SECTION, None),
    )
    out_specs = P(None, FSDP, None, SECTION)
    return jax.shard_map(
        per_device, mesh=split, in_specs=in_specs, out_specs=out_specs, check_vma=False
    )
```

```python
import functools

import jax
import jax.numpy as jnp
from jax import lax
from jax.experimental import pallas as pl
from jax.experimental.pallas import tpu as pltpu
from jax.sharding import Mesh
from jax.sharding import PartitionSpec as P

HEAD_DIM = 128
SPAN_LEN = 64
LAYERS = 8
FEATURES = 2048
SLICE = 256
ACTIVE = 128
EPSILON = 1e-06
FIRST = SPAN_LEN - 1
EARLY = 6

AXES = ("yh", "yl", "xl", "xh", "z", "c")
SIZES = (2, 2, 2, 2, 8, 2)
SECTION = ("yh", "yl", "xl")
FSDP = ("xh", "z", "c")
SWAP = [(0, 1), (1, 0)]


def swapped(block, axis):
    return lax.ppermute(block, axis, SWAP)


def shifted(block, axis, size, distance):
    return lax.ppermute(block, axis, [(i, (i + distance) % size) for i in range(size)])


def gather(block):
    gathered = lax.all_gather(block.reshape(-1, 512), ("z", "c"), axis=0)
    return gathered.reshape((16,) + block.shape)


def flipped(block, axes):
    last = 4 ** (len(axes) // 2) - 1
    return lax.ppermute(block, axes, [(i, last - i) for i in range(last + 1)])


FLIP_Y = ("yh", "yl")
FLIP_X = ("xl", "xh")


def quad(block):
    axis = ("yl", "xl")
    return [lax.ppermute(block, axis, [(i, i ^ d) for i in range(4)]) for d in (1, 2, 3)]


def after(*groups):
    return lax.optimization_barrier(groups)


def kv_kernel(layer_ref, enc_ref, rows_ref, key_ref, value_ref, held, sems):
    layer = layer_ref[0]
    copies = [
        pltpu.make_async_copy(
            rows_ref.at[4 * part : 4 * part + 4, layer, kv, xh],
            held.at[kv, xh, 4 * part : 4 * part + 4],
            sems.at[kv, xh, part],
        )
        for kv in range(2)
        for xh in range(2)
        for part in range(4)
    ]
    for copy in copies:
        copy.start()
    for copy in copies:
        copy.wait()

    def group(g, carry):
        tokens = enc_ref[:, :, pl.ds(2 * g, 2)].reshape(256, 512)
        made = jnp.dot(
            tokens, held[0].reshape(512, 512), preferred_element_type=jnp.float32
        )
        key_ref[g] = made.astype(jnp.bfloat16)
        made = lax.dot_general(
            held[1].reshape(512, 512),
            tokens,
            (((0,), (1,)), ((), ())),
            preferred_element_type=jnp.float32,
        )
        value_ref[g] = made.astype(jnp.bfloat16)
        return carry

    lax.fori_loop(0, 3, group, 0)


def make_kv(encoded, rows, layer):
    vmem = pl.BlockSpec(memory_space=pltpu.VMEM)
    return pl.pallas_call(
        kv_kernel,
        out_shape=(
            jax.ShapeDtypeStruct((3, 256, 512), jnp.bfloat16),
            jax.ShapeDtypeStruct((3, 512, 256), jnp.bfloat16),
        ),
        in_specs=[
            pl.BlockSpec(memory_space=pltpu.SMEM),
            vmem,
            pl.BlockSpec(memory_space=pltpu.HBM),
        ],
        out_specs=(vmem, vmem),
        scratch_shapes=[
            pltpu.VMEM((2, 2, 16, 16, 512), jnp.bfloat16),
            pltpu.SemaphoreType.DMA((2, 2, 4)),
        ],
        compiler_params=pltpu.CompilerParams(vmem_limit_bytes=24 << 20),
        cost_estimate=pl.CostEstimate(
            flops=2 * 768 * 512 * 1024, bytes_accessed=4 << 20, transcendentals=0
        ),
        name="kv",
    )(
        jnp.full((1,), layer, jnp.int32),
        encoded,
        pltpu.with_memory_space_constraint(rows, pltpu.HBM),
    )


SPOT = (0, 1, 3, 5, 7, 6, 4, 2)


def choose_kernel(code_ref, *refs):
    blocks, outs, held = refs[:8], refs[8:10], refs[10]
    for at in range(8):
        held[8 * at : 8 * at + 8] = blocks[at][...]
    for which, out in enumerate(outs):

        def copy(entry, carry, which=which, out=out):
            out[entry] = held[code_ref[which, entry]]
            return carry

        lax.fori_loop(0, 24, copy, 0, unroll=4)


def choose(codes, blocks):
    shape = jax.ShapeDtypeStruct((24, 16, 512), jnp.bfloat16)
    vmem = pl.BlockSpec(memory_space=pltpu.VMEM)
    return pl.pallas_call(
        choose_kernel,
        out_shape=(shape, shape),
        in_specs=[pl.BlockSpec(memory_space=pltpu.SMEM)] + [vmem] * 8,
        out_specs=(vmem, vmem),
        scratch_shapes=[pltpu.VMEM((64, 16, 512), jnp.bfloat16)],
        compiler_params=pltpu.CompilerParams(vmem_limit_bytes=16 << 20),
        name="choose",
    )(codes, *blocks)


def layer_kernel(cur_ref, one_ref, s0_ref, s1_ref, s2_ref, s3_ref, key_ref, value_ref, *outs, last):
    heads = [slice(h * HEAD_DIM, (h + 1) * HEAD_DIM) for h in range(4)]
    queries = [cur_ref[rows, :] for rows in heads]
    own_head = (
        lax.broadcasted_iota(jnp.int32, (512, ACTIVE), 0) // HEAD_DIM
        == lax.broadcasted_iota(jnp.int32, (512, ACTIVE), 1)
    )
    single = one_ref[...].astype(jnp.float32)
    queries_one = jnp.where(own_head, single, 0.0).astype(jnp.bfloat16)
    left = lax.broadcasted_iota(jnp.int32, (1, ACTIVE), 1) < SPAN_LEN

    def dot(first, second):
        return jnp.dot(first, second, preferred_element_type=jnp.float32)

    scores = [
        jnp.where(left, dot(key_ref[0, :, rows], query), dot(key_ref[1, :, rows], query))
        for rows, query in zip(heads, queries)
    ]
    scores.append(dot(key_ref[2], queries_one))
    total = s0_ref[...] + s1_ref[...] + s2_ref[...] + s3_ref[...]
    scale = lax.rsqrt(total * (1.0 / FEATURES) + EPSILON) * HEAD_DIM ** (-0.5)
    scales = [scale[0:1]] * 4 + [scale[1:2]]
    grown = [jnp.exp(score * factor) for score, factor in zip(scores, scales)]
    weights = [
        (one * (1.0 / jnp.sum(one, axis=0, keepdims=True))).astype(jnp.bfloat16) for one in grown
    ]
    mixed = [
        jnp.where(left, dot(value_ref[0, rows, :], weight), dot(value_ref[1, rows, :], weight))
        for rows, weight in zip(heads, weights)
    ]
    mixed_one = dot(value_ref[2], weights[4])
    squares = jnp.zeros((1, ACTIVE), jnp.float32)
    for rows, query, update in zip(heads, queries, mixed):
        made = (query.astype(jnp.float32) + update).astype(jnp.bfloat16)
        wide = made.astype(jnp.float32)
        squares = squares + jnp.sum(wide * wide, axis=0, keepdims=True)
        if last:
            outs[0][0:ACTIVE, rows] = wide.T.astype(jnp.bfloat16)
        else:
            outs[0][rows, :] = made
    mixed_one = jnp.sum(jnp.where(own_head, mixed_one, 0.0), axis=1, keepdims=True)
    made = (single + mixed_one).astype(jnp.bfloat16)
    wide = made.astype(jnp.float32)
    if last:
        outs[0][ACTIVE : ACTIVE + 16, :] = wide.T[0:16].astype(jnp.bfloat16)
    else:
        outs[1][...] = made
        outs[2][0:1, :] = squares
        outs[2][1:2, :] = jnp.sum(wide * wide, axis=0, keepdims=True)


def run_layer(current, single, sums, keys, values, last):
    vmem = pl.BlockSpec(memory_space=pltpu.VMEM)
    if last:
        out_shape = [jax.ShapeDtypeStruct((ACTIVE + 16, 512), jnp.bfloat16)]
    else:
        out_shape = [
            jax.ShapeDtypeStruct((512, ACTIVE), jnp.bfloat16),
            jax.ShapeDtypeStruct((512, ACTIVE), jnp.bfloat16),
            jax.ShapeDtypeStruct((2, ACTIVE), jnp.float32),
        ]
    return pl.pallas_call(
        functools.partial(layer_kernel, last=last),
        out_shape=out_shape,
        in_specs=[vmem] * 8,
        out_specs=[vmem] * len(out_shape),
        compiler_params=pltpu.CompilerParams(vmem_limit_bytes=24 << 20),
        cost_estimate=pl.CostEstimate(
            flops=2 * 20 * 256 * 128 * 128, bytes_accessed=2 << 20, transcendentals=5 * 256 * 128
        ),
        name="layer",
    )(current, single, *sums, keys, values)


def rms_scale(values):
    return values * lax.rsqrt(jnp.mean(values * values, axis=-1, keepdims=True) + EPSILON)


def pick(mask, first, second):
    return jnp.where(mask.reshape(mask.shape + (1, 1)), first, second)


def parts_kernel(key_ref, value_ref, gain_ref, out_ref):
    for label in range(2):
        for xl in range(2):
            for half, y in enumerate((label, 3 - label)):
                spot = 2 * y + xl
                source = slice(spot * SLICE, (spot + 1) * SLICE)
                target = slice(half * SLICE, (half + 1) * SLICE)
                keys = key_ref[0, :, source].astype(jnp.float32) * gain_ref[:, source]
                for section in (2 * label + xl, 2 * (3 - label) + xl):
                    out_ref[section, 0, :, target] = keys.astype(jnp.bfloat16)
                    out_ref[section, 1, :, target] = value_ref[0, :, source]


def weight_parts(key_weight, value_weight, query_gain):
    vmem = pl.BlockSpec(memory_space=pltpu.VMEM)
    return pl.pallas_call(
        parts_kernel,
        out_shape=jax.ShapeDtypeStruct((8, 2, 16, 512), jnp.bfloat16),
        in_specs=[vmem] * 3,
        out_specs=vmem,
        name="parts",
    )(key_weight, value_weight, query_gain)


def per_device(
    hidden, pool_states, neighbour_ids, batch_order, key_weight, value_weight, query_gain
):
    place = {axis: lax.axis_index(axis) for axis in AXES}
    yh, yl, xl, xh, z, c = (place[axis] for axis in AXES)

    is_low = xh == 0
    label = yl ^ yh

    def both_halves(part, other):
        halves = [jnp.where(is_low, part, other), jnp.where(is_low, other, part)]
        return jnp.stack(halves, axis=2)

    def up(block):
        return shifted(block, "z", 8, 1)

    def down(block):
        return shifted(block, "z", 8, -1)

    parts = weight_parts(key_weight, value_weight, query_gain)
    parts, neighbour_ids = after(parts, neighbour_ids)
    rows = lax.all_to_all(parts, SECTION, 0, 0)
    ids = jnp.take(neighbour_ids[:, 0], batch_order, axis=0, mode="clip").reshape(2, 6)
    own = lax.dynamic_index_in_dim(ids, yh, 0, keepdims=False)
    ids = jnp.concatenate([own, lax.dynamic_index_in_dim(ids, 1 - yh, 0, keepdims=False)])
    ids, pool_states = after(ids, pool_states)
    up_1, down_1 = up(pool_states), down(pool_states)
    up_1, down_1, ids, rows = after(up_1, down_1, ids, rows)

    up_2, down_2 = up(up_1), down(down_1)
    rows = both_halves(rows, swapped(rows, "xh"))
    pair = jnp.stack([ids, swapped(ids, "c")])
    opposite = shifted(pool_states, "z", 8, 4)
    up_2, down_2, pair, rows = after(up_2, down_2, pair, rows)
    block, late = rows[:EARLY], rows[EARLY:]

    up_3, down_3 = up(up_2), down(down_2)
    theirs = jnp.concatenate([pair, flipped(pair, FLIP_X)], axis=1)
    codes = jnp.asarray(SPOT, jnp.int32)[(z - (theirs >> 4)) & 7] * 8 + (theirs & 7)
    up_3, down_3, opposite, codes = after(up_3, down_3, opposite, codes)

    early = gather(block)
    pool = [pool_states, up_1, down_1, up_2, down_2, up_3, down_3, opposite]
    kept, sent = choose(codes, pool)
    both = pick(((theirs[0] >> 3) & 1) == c, kept, swapped(sent, "c")).reshape(4, 6, 16, 512)

    from_y, from_x, from_xy = after(
        *(
            flipped(both[part], axes)
            for part, axes in ((1, FLIP_Y), (2, FLIP_X), (3, FLIP_Y + FLIP_X))
        )
    )
    here = (own >> 7) == xh
    tokens = jnp.stack([pick(here, both[0], from_x), pick(here, from_y, from_xy)])
    tokens = rms_scale(tokens.astype(jnp.float32)).astype(jnp.bfloat16)

    tokens, hidden = after(tokens, hidden)
    encoded = jnp.stack([tokens] + quad(tokens))
    ordered = jnp.take(hidden[:, 0], batch_order, axis=0, mode="clip")
    start = lax.dynamic_index_in_dim(ordered, yh, 0, keepdims=False)[FIRST:]
    wide = start.astype(jnp.float32)
    total = jnp.sum(wide * wide, axis=-1)
    sums = jnp.stack([total[:ACTIVE], jnp.broadcast_to(total[ACTIVE:], (ACTIVE,))])
    mine = jnp.concatenate(
        [
            lax.dynamic_slice_in_dim(start, (2 * y + xl) * SLICE, SLICE, 1)
            for y in (label, 3 - label)
        ],
        axis=1,
    )
    current = mine[:ACTIVE].T
    single = jnp.broadcast_to(mine[ACTIVE][:, None], (512, ACTIVE))
    encoded, sums, current, single = after(encoded, sums, current, single)

    nothing = jnp.zeros_like(sums)
    sums = [sums, nothing, nothing, nothing]
    late = gather(late)
    for layer in range(LAYERS):
        last = layer == LAYERS - 1
        if layer < EARLY:
            keys, values = make_kv(encoded, early, layer)
        else:
            keys, values = make_kv(encoded, late, layer - EARLY)
        outs = run_layer(current, single, sums, keys, values, last)
        if not last:
            current, single, partial = outs
            sums = [partial] + quad(partial)
    finished = outs[0].reshape(ACTIVE + 16, 2, SLICE)
    kept = lax.dynamic_index_in_dim(finished, yh, 1, keepdims=False)
    got = flipped(lax.dynamic_index_in_dim(finished, 1 - yh, 1, keepdims=False), FLIP_Y)
    low = yh == 0
    tails = jnp.stack([jnp.where(low, kept, got), jnp.where(low, got, kept)])[:, : ACTIVE + 1]
    heads = lax.dynamic_slice_in_dim(ordered[:, :FIRST], (yh * 4 + yl * 2 + xl) * SLICE, SLICE, 2)
    return jnp.concatenate([heads, tails], axis=1)[:, None]


def solution(mesh):
    split = Mesh(mesh.devices.reshape(SIZES), AXES)
    in_specs = (
        P(None, FSDP, None, None),
        P(FSDP, SECTION, None),
        P(None, FSDP, None, None),
        P(),
        P(SECTION, FSDP, None),
        P(SECTION, FSDP, None),
        P(SECTION, None),
    )
    out_specs = P(None, FSDP, None, SECTION)
    return jax.shard_map(
        per_device, mesh=split, in_specs=in_specs, out_specs=out_specs, check_vma=False
    )
```
